32 devices in a mesh: row: 2 (over core), col: 16 (over z, y, x).
Axes of the slice: x: 2, y: 2, z: 4, core: 2. Of those that a mesh axis runs over, the one named last changes fastest.
Arguments:
- object_re: float32 [512, 4096], P('row', 'col'), may hold values from -6 to 6
- object_im: float32 [512, 4096], P('row', 'col'), may hold values from -6 to 6
- probe_re: float32 [256, 256], replicated, may hold values from -4 to 4
- probe_im: float32 [256, 256], replicated, may hold values from -4 to 4
- intensity: float32 [2, 16, 4, 256, 256], P('row', 'col'), may hold values from 0.05 to 4
- offsets: int32 [2, 16, 4, 2], P('row', 'col'), may hold values from 48 to 208
- counts: int32 [2, 16], P('row', 'col'), may hold values from 2 to 4
Outputs:
- final_re: float32 [512, 4096], P('row', 'col')
- final_im: float32 [512, 4096], P('row', 'col')
The draws below stay inside these ranges and needn't reach their ends.
All inputs are finite; a program needn't handle non-finite values.
Results may differ from the reference program's by a relative error of at most 0.00024.
Values sent between devices are 32-bit elements; how exact they have to be, the bound alone decides.
A program may use at most 64 MiB of HBM per device.

```python
import math
import jax
import jax.numpy as jnp
from jax import lax

W = 256
ITERS = 2
TR = 256
TC = 256
STEP = 128
POS = 4
GRID_R = 2
GRID_C = 16
NR = 512
NC = 4096


def draw_offsets(key, part):
    across = TC // STEP
    jitter_most = STEP // 8
    serial = jnp.arange(POS).astype(jnp.int32)
    base_rows = serial // across * STEP + STEP // 2
    base_cols = serial % across * STEP + STEP // 2
    base = jnp.stack([base_rows, base_cols], axis=1).astype(jnp.int32)
    jitter = jax.random.randint(key, (GRID_R, GRID_C, POS, 2), -jitter_most, jitter_most + 1)
    jitter = jitter.at[0, 0, 0].set(jnp.full((2,), -jitter_most, jnp.int32))
    jitter = jitter.at[GRID_R - 1, GRID_C - 1, POS - 1].set(jnp.full((2,), jitter_most, jnp.int32))
    return (base[None, None] + jitter).astype(jnp.int32)


def draw_counts(key, part):
    values = jax.random.randint(key, (GRID_R, GRID_C), POS // 2, POS + 1)
    values = values.at[0, 0].set(POS // 2)
    values = values.at[GRID_R - 1, GRID_C - 1].set(POS)
    return values.astype(jnp.int32)


def levels(key, shape, cuts, low, high):
    loudness = 1.0
    for position, shards_of in cuts:
        steps = jax.random.uniform(jax.random.fold_in(jax.random.fold_in(key, 6), position), (shards_of,), jnp.float32, low / len(cuts), high / len(cuts))
        loudness = loudness * jnp.repeat(jnp.exp(steps), shape[position] // shards_of).reshape((-1,) + (1,) * (len(shape) - 1 - position))
    return loudness


def bell_draw(stream_key, dims, width, reach, pieces=(), kind=jnp.bfloat16):
    values = width * jax.random.normal(stream_key, dims, jnp.float32)
    if pieces:
        values = values * levels(stream_key, dims, pieces, -0.22, 0.18)
    return jnp.clip(values, -reach, reach).astype(kind)


def setup_inputs(seed: int = 0) -> dict:
    keys = jax.random.split(jax.random.key(seed), 8)
    object_re = bell_draw(keys[0], (NR, NC), 1.0, 6.0, ((0, 2), (1, 16)), jnp.float32)
    object_im = bell_draw(keys[1], (NR, NC), 1.0, 6.0, ((0, 2), (1, 16)), jnp.float32)
    probe_re = bell_draw(keys[2], (W, W), 0.7, 4.0, (), jnp.float32)
    probe_im = bell_draw(keys[3], (W, W), 0.7, 4.0, (), jnp.float32)
    intensity = jnp.clip(jnp.exp(math.log(4.0) - 4.3820266 * jax.random.uniform(keys[4], (GRID_R, GRID_C, POS, W, W), jnp.float32) ** levels(keys[4], (GRID_R, GRID_C, POS, W, W), ((0, 2), (1, 16)), -0.2, 0.2)), 0.05, 4.0)
    offsets = draw_offsets(jax.random.fold_in(keys[7], 71), 0)
    counts = draw_counts(jax.random.fold_in(keys[7], 71), 0)
    return dict(object_re=object_re, object_im=object_im, probe_re=probe_re, probe_im=probe_im, intensity=intensity, offsets=offsets, counts=counts)


smoothing = 0.01
step_size = 0.25

def reference(object_re, object_im, probe_re, probe_im, intensity, offsets, counts):
    margin = W // 2
    probe = lax.complex(probe_re, probe_im)
    total_positions = GRID_R * GRID_C * POS
    serial = jnp.arange(total_positions).astype(jnp.int32)
    tile_row = (serial // (GRID_C * POS)).astype(jnp.int32)
    tile_col = (serial // POS % GRID_C).astype(jnp.int32)
    slot = (serial % POS).astype(jnp.int32)
    flat_offsets = offsets.reshape(total_positions, 2).astype(jnp.int32)
    flat_counts = counts.reshape(GRID_R * GRID_C)
    weights = (slot < flat_counts[serial // POS]).astype(object_re.dtype)
    start_row = (tile_row * TR + flat_offsets[:, 0]).astype(jnp.int32)
    start_col = (tile_col * TC + flat_offsets[:, 1]).astype(jnp.int32)
    measured = intensity.reshape(total_positions, W, W)
    real_part, imag_part = (object_re, object_im)
    for sweep in range(ITERS):
        padded = jnp.pad(jnp.stack([real_part, imag_part]), ((0, 0), (margin, margin), (margin, margin)))

        def visit(gradient, scan_entry):
            leading_row, leading_column, measured_amplitude, update_weight = scan_entry
            corner = (jnp.zeros((), jnp.int32), leading_row, leading_column)
            patch = lax.dynamic_slice(padded, corner, (2, W, W))
            wave = lax.complex(patch[0], patch[1]) * probe
            farfield_wave = jnp.fft.fft2(wave, norm='ortho')
            wave_magnitude = jnp.sqrt(farfield_wave.real * farfield_wave.real + farfield_wave.imag * farfield_wave.imag + smoothing)
            magnitude_error = farfield_wave * (1.0 - jnp.sqrt(measured_amplitude) / wave_magnitude)
            back = jnp.fft.ifft2(magnitude_error, norm='ortho') * jnp.conj(probe)
            term = jnp.stack([back.real, back.imag]) * update_weight
            current = lax.dynamic_slice(gradient, corner, (2, W, W))
            return (lax.dynamic_update_slice(gradient, current + term, corner), None)
        gradient, _ = lax.scan(visit, jnp.zeros_like(padded), (start_row, start_col, measured, weights))
        inner = gradient[:, margin:margin + NR, margin:margin + NC]
        real_part = real_part - step_size * inner[0]
        imag_part = imag_part - step_size * inner[1]
    return (real_part, imag_part)
```

```python
import functools
import math

import jax
import jax.numpy as jnp
import numpy as np
from jax import lax
from jax.experimental import pallas as pl
from jax.experimental.pallas import tpu as pltpu
from jax.sharding import PartitionSpec as P

ITERS = 2
smoothing = 0.01
step_size = 0.25
MESH = pl.DeviceIdType.MESH


def split_tables(length):
    half = length // 2
    n = np.arange(half)
    tables = []
    for odd in (0, 1):
        phase = (2 * n[:, None] + odd) * n[None, :] % length
        angle = phase * (-2.0 * math.pi / length)
        re, im = np.cos(angle) / math.sqrt(length), np.sin(angle) / math.sqrt(length)
        tables.append(np.block([[re, -im], [im, re]]))
    bf16 = jnp.bfloat16
    left, right = [], []
    for table in (tables[0], tables[1], tables[0].T, tables[1].T):
        high = table.astype(np.float32).astype(bf16)
        low = (table - high.astype(np.float64)).astype(np.float32).astype(bf16)
        left.append(np.concatenate([high, high, low], axis=1))
        right.append(np.concatenate([high, high, low], axis=0))
    return np.stack(left), np.stack(right)


def terms(x, axis):
    high = x.astype(jnp.bfloat16)
    low = (x - high.astype(jnp.float32)).astype(jnp.bfloat16)
    return jnp.concatenate([high, low, high], axis=axis)


def mul_left(table, x):
    return jnp.dot(table, terms(x, 0), preferred_element_type=jnp.float32)


def mul_right(x, table):
    return jnp.dot(terms(x, 1), table, preferred_element_type=jnp.float32)


def kernel(
    rows, cols, offsets, counts, object_re, object_im, probe_re, probe_im, intensity, left, right,
    out_re, out_im, ext, grad, probes, roots, picked, turned, from_rows, from_cols, send, recv,
):
    width = probe_re.shape[0]
    half = width // 2
    full = 2 * width
    slots = intensity.shape[0]
    reach = half - half // 2 + half // 8
    inner = slice(half, half + width)
    lo, hi = half - reach, half + width + reach
    row, col = lax.axis_index("row"), lax.axis_index("col")
    there = {
        "up": (row > 0, {"row": row - 1}), "down": (row < rows - 1, {"row": row + 1}),
        "left": (col > 0, {"col": col - 1}), "right": (col < cols - 1, {"col": col + 1}),
    }
    opposite = {"up": "down", "down": "up", "left": "right", "right": "left"}

    ext[...] = jnp.zeros_like(ext)
    ext[0, inner, inner] = object_re[...].T
    ext[1, inner, inner] = object_im[...].T

    barrier = pltpu.get_barrier_semaphore()
    for exists, device in there.values():
        @pl.when(exists)
        def _(device=device):
            pl.semaphore_signal(barrier, inc=1, device_id=device, device_id_type=MESH)
    pl.semaphore_wait(barrier, sum(exists.astype(jnp.int32) for exists, _ in there.values()))

    serial = [0]

    class Send:
        def __init__(self, side, src, dst):
            exists, device = there[side]
            self.out, self.arrives = exists, there[opposite[side]][0]
            self.copy = pltpu.make_async_remote_copy(
                src_ref=src, dst_ref=dst, send_sem=send.at[serial[0]], recv_sem=recv.at[serial[0]],
                device_id=device, device_id_type=MESH,
            )
            serial[0] += 1
            pl.when(self.out)(self.copy.start)

        def received(self):
            pl.when(self.arrives)(self.copy.wait_recv)

        def sent(self):
            pl.when(self.out)(self.copy.wait_send)

    def finish(copies):
        for copy in copies:
            copy.received()
        for copy in copies:
            copy.sent()

    def send_rows(first, last):
        cells = slice(first, last)
        return [
            Send("up", ext.at[:, cells, half : 2 * half], ext.at[:, cells, half + width : full]),
            Send("down", ext.at[:, cells, width : width + half], ext.at[:, cells, 0:half]),
        ]

    sideways = [
        Send("left", ext.at[:, half : half + reach, inner], ext.at[:, half + width : hi, inner]),
        Send("right", ext.at[:, half + width - reach : half + width, inner], ext.at[:, lo:half, inner]),
    ]
    upright = send_rows(half, half + width)

    for p in range(slots):
        down_by = lax.rem(offsets[p, 0] + half, width)
        along_by = lax.rem(offsets[p, 1] + half, width)
        for part, source in enumerate((probe_re, probe_im)):
            moved = pltpu.roll(source[...].T, along_by, 0)
            probes[p, part] = pltpu.roll(moved, down_by, 1)
        for other in (0, 1):
            block = slice(other * half, other * half + half)
            picked[other] = intensity[p, :, block]
        for odd in (0, 1):
            for other in (0, 1):
                block = slice(other * half, other * half + half)
                turned[block, :] = picked[other, pl.ds(odd, half, stride=2), :].T
            for v in (0, 1):
                roots[p, v * half : v * half + half, odd * half : odd * half + half] = jnp.sqrt(
                    turned[pl.ds(v, half, stride=2), :]
                )

    finish(sideways)
    corners = send_rows(lo, half) + send_rows(half + width, hi)
    finish(upright)
    finish(corners)

    across = lax.broadcasted_iota(jnp.int32, (half, full), 0)
    along = lax.broadcasted_iota(jnp.int32, (width, half), 1)

    def own_cells(index, start, cells):
        return cells + half < start + width if index == 0 else cells >= start

    def visit(p):
        a, b = p // 2, p % 2
        top, start = offsets[p, 0] - half, offsets[p, 1] - half
        own_c = own_cells(b, start, across)
        own_r = own_cells(a, top, along)
        used = p < counts[0]

        def patch(part):
            first, second = ext[part, half:width, :], ext[part, width : width + half, :]
            if b == 0:
                second = jnp.where(own_c, second, ext[part, 0:half, :])
            else:
                first = jnp.where(own_c, first, ext[part, half + width : full, :])
            both = jnp.concatenate([first, second], axis=0)
            first, second = both[:, half:width], both[:, width : width + half]
            if a == 0:
                second = jnp.where(own_r, second, both[:, 0:half])
            else:
                first = jnp.where(own_r, first, both[:, half + width : full])
            return jnp.concatenate([first, second], axis=1)

        def place(part, term):
            if a == 0:
                pieces = [jnp.where(own_r, 0.0, term[:, half:]), term[:, :half], jnp.where(own_r, term[:, half:], 0.0)]
                cells = slice(0, half + width)
            else:
                pieces = [jnp.where(own_r, term[:, :half], 0.0), term[:, half:], jnp.where(own_r, 0.0, term[:, :half])]
                cells = slice(half, full)
            term = jnp.concatenate(pieces, axis=1)
            own = own_c[:, : term.shape[1]]
            first, second = term[:half], term[half:]
            if b == 0:
                grad[part, 0:half, cells] += jnp.where(own, 0.0, second)
                second = jnp.where(own, second, 0.0)
            else:
                grad[part, half + width : full, cells] += jnp.where(own, 0.0, first)
                first = jnp.where(own, first, 0.0)
            grad[part, half:width, cells] += first
            grad[part, width : width + half, cells] += second

        cell_re, cell_im = patch(0), patch(1)
        probe_r, probe_i = probes[p, 0], probes[p, 1]
        re = cell_re * probe_r - cell_im * probe_i
        im = cell_re * probe_i + cell_im * probe_r
        even = mul_left(left[0], jnp.concatenate([re[:half] + re[half:], im[:half] + im[half:]], axis=0))
        odd = mul_left(left[1], jnp.concatenate([re[:half] - re[half:], im[:half] - im[half:]], axis=0))
        re = jnp.concatenate([even[:half], odd[:half]], axis=0)
        im = jnp.concatenate([even[half:], odd[half:]], axis=0)
        far = [
            mul_right(jnp.concatenate([re[:, :half] + re[:, half:], im[:, :half] + im[:, half:]], axis=1), right[2]),
            mul_right(jnp.concatenate([re[:, :half] - re[:, half:], im[:, :half] - im[:, half:]], axis=1), right[3]),
        ]
        back = []
        for which, wave in enumerate(far):
            re, im = wave[:, :half], wave[:, half:]
            root = roots[p, :, which * half : which * half + half]
            factor = 1.0 - root * lax.rsqrt(re * re + im * im + smoothing)
            chi = jnp.concatenate([re * factor, im * factor], axis=1)
            back.append(mul_right(chi, right[which]))
        low, high = back[0] + back[1], back[0] - back[1]
        re = jnp.concatenate([low[:, :half], high[:, :half]], axis=1)
        im = jnp.concatenate([low[:, half:], high[:, half:]], axis=1)
        even = mul_left(left[2], jnp.concatenate([re[:half], im[:half]], axis=0))
        odd = mul_left(left[3], jnp.concatenate([re[half:], im[half:]], axis=0))
        low, high = even + odd, even - odd
        re = jnp.concatenate([low[:half], high[:half]], axis=0)
        im = jnp.concatenate([low[half:], high[half:]], axis=0)
        place(0, jnp.where(used, re * probe_r + im * probe_i, 0.0))
        place(1, jnp.where(used, im * probe_r - re * probe_i, 0.0))

    for sweep in range(ITERS):
        grad[...] = jnp.zeros_like(grad)
        for p in range(slots):
            visit(p)

        cells = slice(lo, hi)
        copies = [
            Send("up", grad.at[:, cells, 0:half], from_rows.at[sweep, 1]),
            Send("down", grad.at[:, cells, half + width : full], from_rows.at[sweep, 0]),
        ]
        finish(copies)
        pl.when(there["up"][0])(functools.partial(add, grad, cells, slice(half, 2 * half), from_rows.at[sweep, 0]))
        pl.when(there["down"][0])(functools.partial(add, grad, cells, slice(width, width + half), from_rows.at[sweep, 1]))

        more = sweep < ITERS - 1
        kept = reach if more else 0
        wide = reach + kept
        copies = [
            Send("left", grad.at[:, lo : half + kept, inner], from_cols.at[sweep, 1, :, 0:wide]),
            Send("right", grad.at[:, half + width - kept : hi, inner], from_cols.at[sweep, 0, :, 0:wide]),
        ]
        finish(copies)
        pl.when(there["left"][0])(
            functools.partial(add, grad, slice(half - kept, half + reach), inner, from_cols.at[sweep, 0, :, 0:wide])
        )
        pl.when(there["right"][0])(
            functools.partial(
                add, grad, slice(half + width - reach, half + width + kept), inner, from_cols.at[sweep, 1, :, 0:wide]
            )
        )
        if more:
            new = ext[:, lo:hi, inner] - step_size * grad[:, lo:hi, inner]
            ext[:, half : half + width, inner] = new[:, reach : reach + width]

            @pl.when(there["left"][0])
            def _():
                ext[:, lo:half, inner] = new[:, :reach]

            @pl.when(there["right"][0])
            def _():
                ext[:, half + width : hi, inner] = new[:, reach + width :]

            finish(send_rows(lo, hi))
    out_re[...] = (ext[0, inner, inner] - step_size * grad[0, inner, inner]).T
    out_im[...] = (ext[1, inner, inner] - step_size * grad[1, inner, inner]).T


def add(total, rows, cols, term):
    total[:, rows, cols] += term[...]


def shards(rows, cols, object_re, object_im, probe_re, probe_im, intensity, offsets, counts):
    width = probe_re.shape[0]
    half = width // 2
    reach = half - half // 2 + half // 8
    slots = intensity.shape[2]
    left, right = split_tables(width)
    f32 = jnp.float32
    vmem = pl.BlockSpec(memory_space=pltpu.VMEM)
    smem = pl.BlockSpec(memory_space=pltpu.SMEM)
    tile = jax.ShapeDtypeStruct(object_re.shape, f32)
    return pl.pallas_call(
        functools.partial(kernel, rows, cols),
        out_shape=(tile, tile),
        in_specs=[smem, smem] + [vmem] * 7,
        out_specs=(vmem, vmem),
        scratch_shapes=[
            pltpu.VMEM((2, 2 * width, 2 * width), f32),
            pltpu.VMEM((2, 2 * width, 2 * width), f32),
            pltpu.VMEM((slots, 2, width, width), f32),
            pltpu.VMEM((slots, width, width), f32),
            pltpu.VMEM((2, width, half), f32),
            pltpu.VMEM((width, half), f32),
            pltpu.VMEM((ITERS, 2, 2, width + 2 * reach, half), f32),
            pltpu.VMEM((ITERS, 2, 2, 2 * reach, width), f32),
            pltpu.SemaphoreType.DMA((24,)),
            pltpu.SemaphoreType.DMA((24,)),
        ],
        compiler_params=pltpu.CompilerParams(
            collective_id=0, has_side_effects=True, vmem_limit_bytes=56 * 1024 * 1024
        ),
    )(
        offsets[0, 0], counts[0], object_re, object_im, probe_re, probe_im, intensity[0, 0],
        jnp.asarray(left), jnp.asarray(right),
    )


def solution(mesh):
    return jax.shard_map(
        functools.partial(shards, mesh.shape["row"], mesh.shape["col"]),
        mesh=mesh,
        in_specs=(
            P("row", "col"),
            P("row", "col"),
            P(),
            P(),
            P("row", "col", None, None, None),
            P("row", "col", None, None),
            P("row", "col"),
        ),
        out_specs=(P("row", "col"), P("row", "col")),
        check_vma=False,
    )
```

```python
import functools
import math

import jax
import jax.numpy as jnp
import numpy as np
from jax import lax
from jax.experimental import pallas as pl
from jax.experimental.pallas import tpu as pltpu
from jax.sharding import PartitionSpec as P

ITERS = 2
smoothing = 0.01
step_size = 0.25
MESH = pl.DeviceIdType.MESH


def split_tables(length):
    half = length // 2
    n = np.arange(half)
    tables = []
    for odd in (0, 1):
        phase = (2 * n[:, None] + odd) * n[None, :] % length
        angle = phase * (-2.0 * math.pi / length)
        re, im = np.cos(angle) / math.sqrt(length), np.sin(angle) / math.sqrt(length)
        tables.append(np.block([[re, -im], [im, re]]))
    bf16 = jnp.bfloat16
    left, right = [], []
    for table in (tables[0], tables[1], tables[0].T, tables[1].T):
        high = table.astype(np.float32).astype(bf16)
        low = (table - high.astype(np.float64)).astype(np.float32).astype(bf16)
        left.append(np.concatenate([high, high, low], axis=1))
        right.append(np.concatenate([high, high, low], axis=0))
    return np.stack(left), np.stack(right)


def terms(x, axis):
    high = x.astype(jnp.bfloat16)
    low = (x - high.astype(jnp.float32)).astype(jnp.bfloat16)
    return jnp.concatenate([high, low, high], axis=axis)


def mul_left(table, x):
    return jnp.dot(table, terms(x, 0), preferred_element_type=jnp.float32)


def mul_right(x, table):
    return jnp.dot(terms(x, 1), table, preferred_element_type=jnp.float32)


def kernel(
    rows, cols, offsets, counts, object_re, object_im, probe_re, probe_im, intensity, left, right,
    out_re, out_im, ext, grad, probes, roots, picked, turned, from_rows, from_cols, send, recv,
):
    width = probe_re.shape[0]
    half = width // 2
    full = 2 * width
    slots = intensity.shape[0]
    reach = half - half // 2 + half // 8
    inner = slice(half, half + width)
    lo, hi = half - reach, half + width + reach
    row, col = lax.axis_index("row"), lax.axis_index("col")
    there = {
        "up": (row > 0, {"row": row - 1}), "down": (row < rows - 1, {"row": row + 1}),
        "left": (col > 0, {"col": col - 1}), "right": (col < cols - 1, {"col": col + 1}),
    }
    opposite = {"up": "down", "down": "up", "left": "right", "right": "left"}

    ext[...] = jnp.zeros_like(ext)
    from_rows[...] = jnp.zeros_like(from_rows)
    from_cols[...] = jnp.zeros_like(from_cols)
    grad[...] = jnp.zeros_like(grad)
    ext[0, inner, inner] = object_re[...].T
    ext[1, inner, inner] = object_im[...].T

    barrier = pltpu.get_barrier_semaphore()
    for exists, device in there.values():
        @pl.when(exists)
        def _(device=device):
            pl.semaphore_signal(barrier, inc=1, device_id=device, device_id_type=MESH)
    pl.semaphore_wait(barrier, sum(exists.astype(jnp.int32) for exists, _ in there.values()))

    serial = [0]

    class Send:
        def __init__(self, side, src, dst):
            exists, device = there[side]
            self.out, self.arrives = exists, there[opposite[side]][0]
            self.copy = pltpu.make_async_remote_copy(
                src_ref=src, dst_ref=dst, send_sem=send.at[serial[0]], recv_sem=recv.at[serial[0]],
                device_id=device, device_id_type=MESH,
            )
            serial[0] += 1
            pl.when(self.out)(self.copy.start)

        def received(self):
            pl.when(self.arrives)(self.copy.wait_recv)

        def sent(self):
            pl.when(self.out)(self.copy.wait_send)

    def finish(copies):
        for copy in copies:
            copy.received()
        for copy in copies:
            copy.sent()

    def send_rows(first, last):
        cells = slice(first, last)
        return [
            Send("up", ext.at[:, cells, half : 2 * half], ext.at[:, cells, half + width : full]),
            Send("down", ext.at[:, cells, width : width + half], ext.at[:, cells, 0:half]),
        ]

    rightward = Send("right", ext.at[:, half + width - reach : half + width, inner], ext.at[:, lo:half, inner])
    upright = send_rows(half, half + width)

    for p in range(slots):
        down_by = lax.rem(offsets[p, 0] + half, width)
        along_by = lax.rem(offsets[p, 1] + half, width)
        for part, source in enumerate((probe_re, probe_im)):
            moved = pltpu.roll(source[...].T, along_by, 0)
            probes[p, part] = pltpu.roll(moved, down_by, 1)
        for other in (0, 1):
            block = slice(other * half, other * half + half)
            picked[other] = intensity[p, :, block]
        for odd in (0, 1):
            for other in (0, 1):
                block = slice(other * half, other * half + half)
                turned[block, :] = picked[other, pl.ds(odd, half, stride=2), :].T
            for v in (0, 1):
                roots[p, v * half : v * half + half, odd * half : odd * half + half] = jnp.sqrt(
                    turned[pl.ds(v, half, stride=2), :]
                )

    rightward.sent()
    leftward = Send("left", ext.at[:, half : half + reach, inner], ext.at[:, half + width : hi, inner])
    rightward.received()
    corners = send_rows(lo, half)
    finish(upright + corners)

    across = lax.broadcasted_iota(jnp.int32, (half, full), 0)
    along = lax.broadcasted_iota(jnp.int32, (width, half), 1)

    def own_cells(index, start, cells):
        return cells + half < start + width if index == 0 else cells >= start

    def visit(sweep, p):
        a, b = p // 2, p % 2
        top, start = offsets[p, 0] - half, offsets[p, 1] - half
        own_c = own_cells(b, start, across)
        own_r = own_cells(a, top, along)
        used = p < counts[0]

        def patch(part):
            if b == 0:
                mixed = jnp.where(own_c[:reach], ext[part, width : width + reach, :], ext[part, 0:reach, :])
                pieces = [ext[part, half:width, :], mixed, ext[part, reach:half, :]]
            else:
                mixed = jnp.where(own_c[lo:], ext[part, half + lo : width, :], ext[part, half + width + lo : full, :])
                pieces = [ext[part, half + width : half + width + lo, :], mixed, ext[part, width : width + half, :]]
            both = jnp.concatenate(pieces, axis=0)
            first, second = both[:, half:width], both[:, width : width + half]
            if a == 0:
                second = jnp.where(own_r, second, both[:, 0:half])
            else:
                first = jnp.where(own_r, first, both[:, half + width : full])
            return jnp.concatenate([first, second], axis=1)

        def place(part, term):
            if a == 0:
                pieces = [jnp.where(own_r, 0.0, term[:, half:]), term[:, :half], jnp.where(own_r, term[:, half:], 0.0)]
                cells = slice(0, half + width)
            else:
                pieces = [jnp.where(own_r, term[:, :half], 0.0), term[:, half:], jnp.where(own_r, 0.0, term[:, :half])]
                cells = slice(half, full)
            term = jnp.concatenate(pieces, axis=1)
            own = own_c[:, : term.shape[1]]
            first, second = term[:half], term[half:]
            if b == 0:
                grad[sweep, part, lo:half, cells] += jnp.where(own, 0.0, second)[lo:]
                grad[sweep, part, half:width, cells] += first
                grad[sweep, part, width : width + reach, cells] += jnp.where(own, second, 0.0)[:reach]
            else:
                grad[sweep, part, half + width : hi, cells] += jnp.where(own, 0.0, first)[:reach]
                grad[sweep, part, half + lo : width, cells] += jnp.where(own, first, 0.0)[lo:]
                grad[sweep, part, width : width + half, cells] += second

        cell_re, cell_im = patch(0), patch(1)
        probe_r, probe_i = probes[p, 0], probes[p, 1]
        re = cell_re * probe_r - cell_im * probe_i
        im = cell_re * probe_i + cell_im * probe_r
        even = mul_left(left[0], jnp.concatenate([re[:half] + re[half:], im[:half] + im[half:]], axis=0))
        odd = mul_left(left[1], jnp.concatenate([re[:half] - re[half:], im[:half] - im[half:]], axis=0))
        re = jnp.concatenate([even[:half], odd[:half]], axis=0)
        im = jnp.concatenate([even[half:], odd[half:]], axis=0)
        far = [
            mul_right(jnp.concatenate([re[:, :half] + re[:, half:], im[:, :half] + im[:, half:]], axis=1), right[2]),
            mul_right(jnp.concatenate([re[:, :half] - re[:, half:], im[:, :half] - im[:, half:]], axis=1), right[3]),
        ]
        back = []
        for which, wave in enumerate(far):
            re, im = wave[:, :half], wave[:, half:]
            root = roots[p, :, which * half : which * half + half]
            factor = 1.0 - root * lax.rsqrt(re * re + im * im + smoothing)
            chi = jnp.concatenate([re * factor, im * factor], axis=1)
            back.append(mul_right(chi, right[which]))
        low, high = back[0] + back[1], back[0] - back[1]
        re = jnp.concatenate([low[:, :half], high[:, :half]], axis=1)
        im = jnp.concatenate([low[:, half:], high[:, half:]], axis=1)
        even = mul_left(left[2], jnp.concatenate([re[:half], im[:half]], axis=0))
        odd = mul_left(left[3], jnp.concatenate([re[half:], im[half:]], axis=0))
        low, high = even + odd, even - odd
        re = jnp.concatenate([low[:half], high[:half]], axis=0)
        im = jnp.concatenate([low[half:], high[half:]], axis=0)
        place(0, jnp.where(used, re * probe_r + im * probe_i, 0.0))
        place(1, jnp.where(used, im * probe_r - re * probe_i, 0.0))

    def start_rows(sweep, first, last):
        cells, slot = slice(first, last), slice(first - lo, last - lo)
        return [
            Send("up", grad.at[sweep, :, cells, 0:half], from_rows.at[sweep, 1, :, slot]),
            Send("down", grad.at[sweep, :, cells, half + width : full], from_rows.at[sweep, 0, :, slot]),
        ]

    def end_rows(sweep, first, last, copies):
        cells, slot = slice(first, last), slice(first - lo, last - lo)
        finish(copies)
        grad[sweep, :, cells, half:width] += from_rows[sweep, 0, :, slot]
        grad[sweep, :, cells, width : width + half] += from_rows[sweep, 1, :, slot]

    def start_side(sweep, side, first, last, slot):
        landing = from_cols.at[sweep, 1 if side == "left" else 0, :, slot : slot + last - first]
        return Send(side, grad.at[sweep, :, first:last, inner], landing)

    def step(sweep, first, last, exists=None, term=None):
        total = grad[sweep, :, first:last, inner]
        if term is not None:
            total = total + term
        new = ext[:, first:last, inner] - step_size * total
        return new if exists is None else jnp.where(exists, new, 0.0)

    split_lo, split_hi = half + lo, width + reach
    near = half + reach
    far_in = half + width - reach
    here_left, here_right = there["left"][0], there["right"][0]
    left_slots = [p for p in range(slots) if p % 2 == 0]
    right_slots = [p for p in range(slots) if p % 2 == 1]

    visit(0, left_slots[0])
    leftward.received()
    corners = send_rows(half + width, hi)
    for p in left_slots[1:]:
        visit(0, p)
    early_rows = start_rows(0, lo, split_lo)
    finish(corners)
    visit(0, right_slots[0])
    end_rows(0, lo, split_lo, early_rows)
    left_main = start_side(0, "left", lo, split_lo, 0)
    for p in right_slots[1:]:
        visit(0, p)
    end_rows(0, split_lo, hi, start_rows(0, split_lo, hi))
    left_rest = start_side(0, "left", split_lo, near, half)
    right_rest = start_side(0, "right", far_in + half, hi, half)
    right_main = start_side(0, "right", far_in, far_in + half, 0)
    leftward.sent()
    left_main.received()
    left_rest.received()
    right_rest.received()
    ext[:, split_lo:near, inner] = step(0, split_lo, near, None, from_cols[0, 0, :, half : 2 * reach])
    ext[:, near:far_in, inner] = step(0, near, far_in)
    ext[:, far_in : half + width, inner] = step(0, far_in, half + width, None, from_cols[0, 1, :, 0:reach])
    ext[:, half + width : hi, inner] = step(0, half + width, hi, here_right, from_cols[0, 1, :, reach : 2 * reach])
    finish(send_rows(split_lo, hi))

    visit(1, right_slots[0])
    right_main.received()
    ext[:, lo:half, inner] = step(0, lo, half, here_left, from_cols[0, 0, :, 0:reach])
    ext[:, half:split_lo, inner] = step(0, half, split_lo, None, from_cols[0, 0, :, reach:half])
    upright = send_rows(lo, split_lo)
    for p in right_slots[1:]:
        visit(1, p)
    late_rows = start_rows(1, split_hi, hi)
    finish(upright)
    visit(1, left_slots[0])
    end_rows(1, split_hi, hi, late_rows)
    right_last = start_side(1, "right", half + width, hi, 0)
    for p in left_slots[1:]:
        visit(1, p)
    end_rows(1, lo, split_hi, start_rows(1, lo, split_hi))
    left_last = start_side(1, "left", lo, half, 0)
    for part in (0, 1):
        ext[part, near:far_in, inner] -= step_size * grad[1, part, near:far_in, inner]
    right_last.received()
    ext[:, half:near, inner] = step(1, half, near, None, from_cols[1, 0, :, 0:reach])
    left_last.received()
    ext[:, far_in : half + width, inner] = step(1, far_in, half + width, None, from_cols[1, 1, :, 0:reach])
    out_re[...] = ext[0, inner, inner].T
    out_im[...] = ext[1, inner, inner].T
    for copy in (left_main, left_rest, right_rest, right_main, right_last, left_last):
        copy.sent()


def shards(rows, cols, object_re, object_im, probe_re, probe_im, intensity, offsets, counts):
    width = probe_re.shape[0]
    half = width // 2
    reach = half - half // 2 + half // 8
    slots = intensity.shape[2]
    left, right = split_tables(width)
    f32 = jnp.float32
    vmem = pl.BlockSpec(memory_space=pltpu.VMEM)
    smem = pl.BlockSpec(memory_space=pltpu.SMEM)
    tile = jax.ShapeDtypeStruct(object_re.shape, f32)
    return pl.pallas_call(
        functools.partial(kernel, rows, cols),
        out_shape=(tile, tile),
        in_specs=[smem, smem] + [vmem] * 7,
        out_specs=(vmem, vmem),
        scratch_shapes=[
            pltpu.VMEM((2, 2 * width, 2 * width), f32),
            pltpu.VMEM((ITERS, 2, 2 * width, 2 * width), f32),
            pltpu.VMEM((slots, 2, width, width), f32),
            pltpu.VMEM((slots, width, width), f32),
            pltpu.VMEM((2, width, half), f32),
            pltpu.VMEM((width, half), f32),
            pltpu.VMEM((ITERS, 2, 2, width + 2 * reach, half), f32),
            pltpu.VMEM((ITERS, 2, 2, 2 * reach, width), f32),
            pltpu.SemaphoreType.DMA((32,)),
            pltpu.SemaphoreType.DMA((32,)),
        ],
        compiler_params=pltpu.CompilerParams(
            collective_id=0, has_side_effects=True, vmem_limit_bytes=56 * 1024 * 1024
        ),
    )(
        offsets[0, 0], counts[0], object_re, object_im, probe_re, probe_im, intensity[0, 0],
        jnp.asarray(left), jnp.asarray(right),
    )


def solution(mesh):
    return jax.shard_map(
        functools.partial(shards, mesh.shape["row"], mesh.shape["col"]),
        mesh=mesh,
        in_specs=(
            P("row", "col"),
            P("row", "col"),
            P(),
            P(),
            P("row", "col", None, None, None),
            P("row", "col", None, None),
            P("row", "col"),
        ),
        out_specs=(P("row", "col"), P("row", "col")),
        check_vma=False,
    )
```

```python
import functools
import math

import jax
import jax.numpy as jnp
import numpy as np
from jax import lax
from jax.experimental import pallas as pl
from jax.experimental.pallas import tpu as pltpu
from jax.sharding import PartitionSpec as P

ITERS = 2
smoothing = 0.01
step_size = 0.25
MESH = pl.DeviceIdType.MESH


def split_tables(length):
    half = length // 2
    n = np.arange(half)
    tables = []
    for odd in (0, 1):
        phase = (2 * n[:, None] + odd) * n[None, :] % length
        angle = phase * (-2.0 * math.pi / length)
        re, im = np.cos(angle) / math.sqrt(length), np.sin(angle) / math.sqrt(length)
        tables.append(np.block([[re, -im], [im, re]]))
    bf16 = jnp.bfloat16
    left, right = [], []
    for table in (tables[0], tables[1], tables[0].T, tables[1].T):
        high = table.astype(np.float32).astype(bf16)
        low = (table - high.astype(np.float64)).astype(np.float32).astype(bf16)
        left.append(np.concatenate([high, high, low], axis=1))
        right.append(np.concatenate([high, high, low], axis=0))
    return np.stack(left), np.stack(right)


def terms(x, axis):
    high = x.astype(jnp.bfloat16)
    low = (x - high.astype(jnp.float32)).astype(jnp.bfloat16)
    return jnp.concatenate([high, low, high], axis=axis)


def mul_left(table, x):
    return jnp.dot(table, terms(x, 0), preferred_element_type=jnp.float32)


def mul_right(x, table):
    return jnp.dot(terms(x, 1), table, preferred_element_type=jnp.float32)


def kernel(
    rows, cols, offsets, counts, object_re, object_im, probe_re, probe_im, stored_i, stored_l, stored_r,
    out_re, out_im, ext, grad, probes, roots, picked, turned, from_rows, from_cols,
    intensity, left, right, send, recv, load,
):
    width = probe_re.shape[0]
    half = width // 2
    full = 2 * width
    slots = intensity.shape[0]
    reach = half - half // 2 + half // 8
    inner = slice(half, half + width)
    lo, hi = half - reach, half + width + reach
    row, col = lax.axis_index("row"), lax.axis_index("col")
    there = {
        "up": (row > 0, {"row": row - 1}), "down": (row < rows - 1, {"row": row + 1}),
        "left": (col > 0, {"col": col - 1}), "right": (col < cols - 1, {"col": col + 1}),
    }
    opposite = {"up": "down", "down": "up", "left": "right", "right": "left"}

    loads = [
        pltpu.make_async_copy(src, dst, load.at[k])
        for k, (src, dst) in enumerate(((stored_i, intensity), (stored_l, left), (stored_r, right)))
    ]
    for copy in loads:
        copy.start()
    ext[...] = jnp.zeros_like(ext)
    ext[0, inner, inner] = object_re[...].T
    ext[1, inner, inner] = object_im[...].T

    for landing, sides in ((from_rows, ("up", "down")), (from_cols, ("left", "right"))):
        for k, side in enumerate(sides):
            @pl.when(jnp.logical_not(there[side][0]))
            def _(landing=landing, k=k):
                landing[:, k] = jnp.zeros(landing.shape[:1] + landing.shape[2:], jnp.float32)

    barrier = pltpu.get_barrier_semaphore()
    for exists, device in there.values():
        @pl.when(exists)
        def _(device=device):
            pl.semaphore_signal(barrier, inc=1, device_id=device, device_id_type=MESH)
    pl.semaphore_wait(barrier, sum(exists.astype(jnp.int32) for exists, _ in there.values()))

    serial = [0]

    class Send:
        def __init__(self, side, src, dst):
            exists, device = there[side]
            self.out, self.arrives = exists, there[opposite[side]][0]
            self.copy = pltpu.make_async_remote_copy(
                src_ref=src, dst_ref=dst, send_sem=send.at[serial[0]], recv_sem=recv.at[serial[0]],
                device_id=device, device_id_type=MESH,
            )
            serial[0] += 1
            pl.when(self.out)(self.copy.start)

        def received(self):
            pl.when(self.arrives)(self.copy.wait_recv)

        def sent(self):
            pl.when(self.out)(self.copy.wait_send)

    def finish(copies):
        for copy in copies:
            copy.received()
        for copy in copies:
            copy.sent()

    def send_rows(first, last):
        cells = slice(first, last)
        return [
            Send("up", ext.at[:, cells, half : 2 * half], ext.at[:, cells, half + width : full]),
            Send("down", ext.at[:, cells, width : width + half], ext.at[:, cells, 0:half]),
        ]

    rightward = Send("right", ext.at[:, half + width - reach : half + width, inner], ext.at[:, lo:half, inner])
    upright = send_rows(half, half + width)

    grad[...] = jnp.zeros_like(grad)
    loads[0].wait()
    for p in range(slots):
        down_by = lax.rem(offsets[p, 0] + half, width)
        along_by = lax.rem(offsets[p, 1] + half, width)
        for part, source in enumerate((probe_re, probe_im)):
            moved = pltpu.roll(source[...].T, along_by, 0)
            probes[p, part] = pltpu.roll(moved, down_by, 1)
        for other in (0, 1):
            block = slice(other * half, other * half + half)
            picked[other] = intensity[p, :, block]
        for odd in (0, 1):
            for other in (0, 1):
                block = slice(other * half, other * half + half)
                turned[block, :] = picked[other, pl.ds(odd, half, stride=2), :].T
            for v in (0, 1):
                roots[p, v * half : v * half + half, odd * half : odd * half + half] = jnp.sqrt(
                    turned[pl.ds(v, half, stride=2), :]
                )

    loads[1].wait()
    loads[2].wait()
    rightward.sent()
    leftward = Send("left", ext.at[:, half : half + reach, inner], ext.at[:, half + width : hi, inner])
    rightward.received()
    corners = send_rows(lo, half)
    finish(upright + corners)

    across = lax.broadcasted_iota(jnp.int32, (half, full), 0)
    along = lax.broadcasted_iota(jnp.int32, (width, half), 1)

    def own_cells(index, start, cells):
        return cells + half < start + width if index == 0 else cells >= start

    def visit(sweep, p):
        a, b = p // 2, p % 2
        top, start = offsets[p, 0] - half, offsets[p, 1] - half
        own_c = own_cells(b, start, across)
        own_r = own_cells(a, top, along)
        used = p < counts[0]

        def patch(part):
            if b == 0:
                mixed = jnp.where(own_c[:reach], ext[part, width : width + reach, :], ext[part, 0:reach, :])
                pieces = [ext[part, half:width, :], mixed, ext[part, reach:half, :]]
            else:
                mixed = jnp.where(own_c[lo:], ext[part, half + lo : width, :], ext[part, half + width + lo : full, :])
                pieces = [ext[part, half + width : half + width + lo, :], mixed, ext[part, width : width + half, :]]
            both = jnp.concatenate(pieces, axis=0)
            first, second = both[:, half:width], both[:, width : width + half]
            if a == 0:
                second = jnp.where(own_r, second, both[:, 0:half])
            else:
                first = jnp.where(own_r, first, both[:, half + width : full])
            return jnp.concatenate([first, second], axis=1)

        def place(part, term):
            if a == 0:
                pieces = [jnp.where(own_r, 0.0, term[:, half:]), term[:, :half], jnp.where(own_r, term[:, half:], 0.0)]
                cells = slice(0, half + width)
            else:
                pieces = [jnp.where(own_r, term[:, :half], 0.0), term[:, half:], jnp.where(own_r, 0.0, term[:, :half])]
                cells = slice(half, full)
            term = jnp.concatenate(pieces, axis=1)
            own = own_c[:, : term.shape[1]]
            first, second = term[:half], term[half:]
            if b == 0:
                grad[sweep, part, lo:half, cells] += jnp.where(own, 0.0, second)[lo:]
                grad[sweep, part, half:width, cells] += first
                grad[sweep, part, width : width + reach, cells] += jnp.where(own, second, 0.0)[:reach]
            else:
                grad[sweep, part, half + width : hi, cells] += jnp.where(own, 0.0, first)[:reach]
                grad[sweep, part, half + lo : width, cells] += jnp.where(own, first, 0.0)[lo:]
                grad[sweep, part, width : width + half, cells] += second

        cell_re, cell_im = patch(0), patch(1)
        probe_r, probe_i = probes[p, 0], probes[p, 1]
        re = cell_re * probe_r - cell_im * probe_i
        im = cell_re * probe_i + cell_im * probe_r
        even = mul_left(left[0], jnp.concatenate([re[:half] + re[half:], im[:half] + im[half:]], axis=0))
        odd = mul_left(left[1], jnp.concatenate([re[:half] - re[half:], im[:half] - im[half:]], axis=0))
        re = jnp.concatenate([even[:half], odd[:half]], axis=0)
        im = jnp.concatenate([even[half:], odd[half:]], axis=0)
        far = [
            mul_right(jnp.concatenate([re[:, :half] + re[:, half:], im[:, :half] + im[:, half:]], axis=1), right[2]),
            mul_right(jnp.concatenate([re[:, :half] - re[:, half:], im[:, :half] - im[:, half:]], axis=1), right[3]),
        ]
        back = []
        for which, wave in enumerate(far):
            re, im = wave[:, :half], wave[:, half:]
            root = roots[p, :, which * half : which * half + half]
            factor = 1.0 - root * lax.rsqrt(re * re + im * im + smoothing)
            chi = jnp.concatenate([re * factor, im * factor], axis=1)
            back.append(mul_right(chi, right[which]))
        low, high = back[0] + back[1], back[0] - back[1]
        re = jnp.concatenate([low[:, :half], high[:, :half]], axis=1)
        im = jnp.concatenate([low[:, half:], high[:, half:]], axis=1)
        even = mul_left(left[2], jnp.concatenate([re[:half], im[:half]], axis=0))
        odd = mul_left(left[3], jnp.concatenate([re[half:], im[half:]], axis=0))
        low, high = even + odd, even - odd
        re = jnp.concatenate([low[:half], high[:half]], axis=0)
        im = jnp.concatenate([low[half:], high[half:]], axis=0)
        place(0, jnp.where(used, re * probe_r + im * probe_i, 0.0))
        place(1, jnp.where(used, im * probe_r - re * probe_i, 0.0))

    def start_rows(sweep, first, last):
        cells, slot = slice(first, last), slice(first - lo, last - lo)
        return [
            Send("up", grad.at[sweep, :, cells, 0:half], from_rows.at[sweep, 1, :, slot]),
            Send("down", grad.at[sweep, :, cells, half + width : full], from_rows.at[sweep, 0, :, slot]),
        ]

    def end_rows(sweep, first, last, copies):
        cells, slot = slice(first, last), slice(first - lo, last - lo)
        finish(copies)
        grad[sweep, :, cells, half:width] += from_rows[sweep, 0, :, slot]
        grad[sweep, :, cells, width : width + half] += from_rows[sweep, 1, :, slot]

    def start_side(sweep, side, first, last, slot):
        landing = from_cols.at[sweep, 1 if side == "left" else 0, :, slot : slot + last - first]
        return Send(side, grad.at[sweep, :, first:last, inner], landing)

    def step(sweep, first, last, exists=None, term=None):
        total = grad[sweep, :, first:last, inner]
        if term is not None:
            total = total + term
        new = ext[:, first:last, inner] - step_size * total
        return new if exists is None else jnp.where(exists, new, 0.0)

    split_lo, split_hi = half + lo, width + reach
    near = half + reach
    far_in = half + width - reach
    here_left, here_right = there["left"][0], there["right"][0]
    left_slots = [p for p in range(slots) if p % 2 == 0]
    right_slots = [p for p in range(slots) if p % 2 == 1]

    visit(0, left_slots[0])
    leftward.received()
    corners = send_rows(half + width, hi)
    for p in left_slots[1:]:
        visit(0, p)
    early_rows = start_rows(0, lo, split_lo)
    finish(corners)
    visit(0, right_slots[0])
    end_rows(0, lo, split_lo, early_rows)
    left_main = start_side(0, "left", lo, split_lo, 0)
    for p in right_slots[1:]:
        visit(0, p)
    end_rows(0, split_lo, hi, start_rows(0, split_lo, hi))
    left_rest = start_side(0, "left", split_lo, near, half)
    right_rest = start_side(0, "right", far_in + half, hi, half)
    right_main = start_side(0, "right", far_in, far_in + half, 0)
    leftward.sent()
    left_main.received()
    left_rest.received()
    right_rest.received()
    ext[:, split_lo:near, inner] = step(0, split_lo, near, None, from_cols[0, 0, :, half : 2 * reach])
    ext[:, near:far_in, inner] = step(0, near, far_in)
    ext[:, far_in : half + width, inner] = step(0, far_in, half + width, None, from_cols[0, 1, :, 0:reach])
    ext[:, half + width : hi, inner] = step(0, half + width, hi, here_right, from_cols[0, 1, :, reach : 2 * reach])
    finish(send_rows(split_lo, hi))

    visit(1, right_slots[0])
    right_main.received()
    ext[:, lo:half, inner] = step(0, lo, half, here_left, from_cols[0, 0, :, 0:reach])
    ext[:, half:split_lo, inner] = step(0, half, split_lo, None, from_cols[0, 0, :, reach:half])
    upright = send_rows(lo, split_lo)
    for p in right_slots[1:]:
        visit(1, p)
    late_rows = start_rows(1, split_hi, hi)
    finish(upright)
    visit(1, left_slots[0])
    end_rows(1, split_hi, hi, late_rows)
    right_last = start_side(1, "right", half + width, hi, 0)
    for p in left_slots[1:]:
        visit(1, p)
    end_rows(1, lo, split_hi, start_rows(1, lo, split_hi))
    left_last = start_side(1, "left", lo, half, 0)
    for part in (0, 1):
        ext[part, near:far_in, inner] -= step_size * grad[1, part, near:far_in, inner]
    right_last.received()
    ext[:, half:near, inner] = step(1, half, near, None, from_cols[1, 0, :, 0:reach])
    left_last.received()
    ext[:, far_in : half + width, inner] = step(1, far_in, half + width, None, from_cols[1, 1, :, 0:reach])
    out_re[...] = ext[0, inner, inner]
    out_im[...] = ext[1, inner, inner]
    for copy in (left_main, left_rest, right_rest, right_main, right_last, left_last):
        copy.sent()


def turn(turned_re, turned_im, final_re, final_im):
    final_re[...] = turned_re[...].T
    final_im[...] = turned_im[...].T


def shards(rows, cols, object_re, object_im, probe_re, probe_im, intensity, offsets, counts):
    width = probe_re.shape[0]
    half = width // 2
    reach = half - half // 2 + half // 8
    slots = intensity.shape[2]
    left, right = split_tables(width)
    f32 = jnp.float32
    vmem = pl.BlockSpec(memory_space=pltpu.VMEM)
    smem = pl.BlockSpec(memory_space=pltpu.SMEM)
    tile = jax.ShapeDtypeStruct(object_re.shape, f32)
    turned = jax.ShapeDtypeStruct(object_re.shape[::-1], f32)
    turned_re, turned_im = pl.pallas_call(
        functools.partial(kernel, rows, cols),
        out_shape=(turned, turned),
        in_specs=[smem, smem] + [vmem] * 4 + [pl.BlockSpec(memory_space=pl.ANY)] * 3,
        out_specs=(vmem, vmem),
        scratch_shapes=[
            pltpu.VMEM((2, 2 * width, 2 * width), f32),
            pltpu.VMEM((ITERS, 2, 2 * width, 2 * width), f32),
            pltpu.VMEM((slots, 2, width, width), f32),
            pltpu.VMEM((slots, width, width), f32),
            pltpu.VMEM((2, width, half), f32),
            pltpu.VMEM((width, half), f32),
            pltpu.VMEM((ITERS, 2, 2, width + 2 * reach, half), f32),
            pltpu.VMEM((ITERS, 2, 2, 2 * reach, width), f32),
            pltpu.VMEM(intensity.shape[2:], f32),
            pltpu.VMEM(left.shape, jnp.bfloat16),
            pltpu.VMEM(right.shape, jnp.bfloat16),
            pltpu.SemaphoreType.DMA((32,)),
            pltpu.SemaphoreType.DMA((32,)),
            pltpu.SemaphoreType.DMA((3,)),
        ],
        compiler_params=pltpu.CompilerParams(
            collective_id=0, has_side_effects=True, vmem_limit_bytes=56 * 1024 * 1024
        ),
    )(
        offsets[0, 0], counts[0], object_re, object_im, probe_re, probe_im, intensity[0, 0],
        jnp.asarray(left), jnp.asarray(right),
    )
    return pl.pallas_call(turn, out_shape=(tile, tile), in_specs=[vmem] * 2, out_specs=(vmem, vmem))(
        turned_re, turned_im
    )


def solution(mesh):
    return jax.shard_map(
        functools.partial(shards, mesh.shape["row"], mesh.shape["col"]),
        mesh=mesh,
        in_specs=(
            P("row", "col"),
            P("row", "col"),
            P(),
            P(),
            P("row", "col", None, None, None),
            P("row", "col", None, None),
            P("row", "col"),
        ),
        out_specs=(P("row", "col"), P("row", "col")),
        check_vma=False,
    )
```

```python
import functools
import math

import jax
import jax.numpy as jnp
import numpy as np
from jax import lax
from jax.experimental import pallas as pl
from jax.experimental.pallas import tpu as pltpu
from jax.sharding import PartitionSpec as P

ITERS = 2
smoothing = 0.01
step_size = 0.25
MESH = pl.DeviceIdType.MESH


def split_tables(length):
    half = length // 2
    n = np.arange(half)
    tables = []
    for odd in (0, 1):
        phase = (2 * n[:, None] + odd) * n[None, :] % length
        angle = phase * (-2.0 * math.pi / length)
        re, im = np.cos(angle) / math.sqrt(length), np.sin(angle) / math.sqrt(length)
        tables.append(np.block([[re, -im], [im, re]]))
    bf16 = jnp.bfloat16
    left, right = [], []
    for table in (tables[0], tables[1], tables[0].T, tables[1].T):
        high = table.astype(np.float32).astype(bf16)
        low = (table - high.astype(np.float64)).astype(np.float32).astype(bf16)
        left.append(np.concatenate([high, high, low], axis=1))
        right.append(np.concatenate([high, high, low], axis=0))
    return np.stack(left), np.stack(right)


def terms(x, axis):
    high = x.astype(jnp.bfloat16)
    low = (x - high.astype(jnp.float32)).astype(jnp.bfloat16)
    return jnp.concatenate([high, low, high], axis=axis)


def mul_left(table, x):
    return jnp.dot(table, terms(x, 0), preferred_element_type=jnp.float32)


def mul_right(x, table):
    return jnp.dot(terms(x, 1), table, preferred_element_type=jnp.float32)


def kernel(
    rows, cols, offsets, counts, object_re, object_im, probe_re, probe_im, stored_i, stored_l, stored_r,
    out_re, out_im, ext, grad, probes, roots, picked, turned, from_rows, from_cols,
    intensity, left, right, send, recv, load,
):
    width = probe_re.shape[0]
    half = width // 2
    full = 2 * width
    slots = intensity.shape[0]
    reach = half - half // 2 + half // 8
    inner = slice(half, half + width)
    lo, hi = half - reach, half + width + reach
    row, col = lax.axis_index("row"), lax.axis_index("col")
    there = {
        "up": (row > 0, {"row": row - 1}), "down": (row < rows - 1, {"row": row + 1}),
        "left": (col > 0, {"col": col - 1}), "right": (col < cols - 1, {"col": col + 1}),
    }
    opposite = {"up": "down", "down": "up", "left": "right", "right": "left"}

    loads = [
        pltpu.make_async_copy(src, dst, load.at[k])
        for k, (src, dst) in enumerate(((stored_i, intensity), (stored_l, left), (stored_r, right)))
    ]
    for copy in loads:
        copy.start()
    ext[...] = jnp.zeros_like(ext)
    ext[0, inner, inner] = object_re[...].T
    ext[1, inner, inner] = object_im[...].T

    for landing, sides in ((from_rows, ("up", "down")), (from_cols, ("left", "right"))):
        for k, side in enumerate(sides):
            @pl.when(jnp.logical_not(there[side][0]))
            def _(landing=landing, k=k):
                landing[:, k] = jnp.zeros(landing.shape[:1] + landing.shape[2:], jnp.float32)

    barrier = pltpu.get_barrier_semaphore()
    for exists, device in there.values():
        @pl.when(exists)
        def _(device=device):
            pl.semaphore_signal(barrier, inc=1, device_id=device, device_id_type=MESH)
    pl.semaphore_wait(barrier, sum(exists.astype(jnp.int32) for exists, _ in there.values()))

    serial = [0]

    class Send:
        def __init__(self, side, src, dst):
            exists, device = there[side]
            self.out, self.arrives = exists, there[opposite[side]][0]
            self.copy = pltpu.make_async_remote_copy(
                src_ref=src, dst_ref=dst, send_sem=send.at[serial[0]], recv_sem=recv.at[serial[0]],
                device_id=device, device_id_type=MESH,
            )
            serial[0] += 1
            pl.when(self.out)(self.copy.start)

        def received(self):
            pl.when(self.arrives)(self.copy.wait_recv)

        def sent(self):
            pl.when(self.out)(self.copy.wait_send)

    def finish(copies):
        for copy in copies:
            copy.received()
        for copy in copies:
            copy.sent()

    def send_rows(first, last):
        cells = slice(first, last)
        return [
            Send("up", ext.at[:, cells, half : 2 * half], ext.at[:, cells, half + width : full]),
            Send("down", ext.at[:, cells, width : width + half], ext.at[:, cells, 0:half]),
        ]

    rightward = Send("right", ext.at[:, half + width - reach : half + width, inner], ext.at[:, lo:half, inner])
    upright = send_rows(half, half + width)

    grad[...] = jnp.zeros_like(grad)
    loads[0].wait()
    for p in range(slots):
        down_by = lax.rem(offsets[p, 0] + half, width)
        along_by = lax.rem(offsets[p, 1] + half, width)
        for part, source in enumerate((probe_re, probe_im)):
            moved = pltpu.roll(source[...].T, along_by, 0)
            probes[p, part] = pltpu.roll(moved, down_by, 1)
        for other in (0, 1):
            block = slice(other * half, other * half + half)
            picked[other] = intensity[p, :, block]
        for odd in (0, 1):
            for other in (0, 1):
                block = slice(other * half, other * half + half)
                turned[block, :] = picked[other, pl.ds(odd, half, stride=2), :].T
            for v in (0, 1):
                roots[p, v * half : v * half + half, odd * half : odd * half + half] = jnp.sqrt(
                    turned[pl.ds(v, half, stride=2), :]
                )

    loads[1].wait()
    loads[2].wait()
    rightward.sent()
    leftward = Send("left", ext.at[:, half : half + reach, inner], ext.at[:, half + width : hi, inner])
    rightward.received()
    corners = send_rows(lo, half)
    finish(upright + corners)

    across = lax.broadcasted_iota(jnp.int32, (half, full), 0)
    along = lax.broadcasted_iota(jnp.int32, (width, half), 1)

    def own_cells(index, start, cells):
        return cells + half < start + width if index == 0 else cells >= start

    def visit(sweep, p):
        a, b = p // 2, p % 2
        top, start = offsets[p, 0] - half, offsets[p, 1] - half
        own_c = own_cells(b, start, across)
        own_r = own_cells(a, top, along)
        used = p < counts[0]

        def patch(part):
            if b == 0:
                mixed = jnp.where(own_c[:reach], ext[part, width : width + reach, :], ext[part, 0:reach, :])
                pieces = [ext[part, half:width, :], mixed, ext[part, reach:half, :]]
            else:
                mixed = jnp.where(own_c[lo:], ext[part, half + lo : width, :], ext[part, half + width + lo : full, :])
                pieces = [ext[part, half + width : half + width + lo, :], mixed, ext[part, width : width + half, :]]
            both = jnp.concatenate(pieces, axis=0)
            first, second = both[:, half:width], both[:, width : width + half]
            if a == 0:
                second = jnp.where(own_r, second, both[:, 0:half])
            else:
                first = jnp.where(own_r, first, both[:, half + width : full])
            return jnp.concatenate([first, second], axis=1)

        def place(part, term):
            if a == 0:
                pieces = [jnp.where(own_r, 0.0, term[:, half:]), term[:, :half], jnp.where(own_r, term[:, half:], 0.0)]
                cells = slice(0, half + width)
            else:
                pieces = [jnp.where(own_r, term[:, :half], 0.0), term[:, half:], jnp.where(own_r, 0.0, term[:, :half])]
                cells = slice(half, full)
            term = jnp.concatenate(pieces, axis=1)
            own = own_c[:, : term.shape[1]]
            first, second = term[:half], term[half:]
            if b == 0:
                grad[sweep, part, lo:half, cells] += jnp.where(own, 0.0, second)[lo:]
                grad[sweep, part, half:width, cells] += first
                grad[sweep, part, width : width + reach, cells] += jnp.where(own, second, 0.0)[:reach]
            else:
                grad[sweep, part, half + width : hi, cells] += jnp.where(own, 0.0, first)[:reach]
                grad[sweep, part, half + lo : width, cells] += jnp.where(own, first, 0.0)[lo:]
                grad[sweep, part, width : width + half, cells] += second

        cell_re, cell_im = patch(0), patch(1)
        probe_r, probe_i = probes[p, 0], probes[p, 1]
        re = cell_re * probe_r - cell_im * probe_i
        im = cell_re * probe_i + cell_im * probe_r
        even = mul_left(left[0], jnp.concatenate([re[:half] + re[half:], im[:half] + im[half:]], axis=0))
        odd = mul_left(left[1], jnp.concatenate([re[:half] - re[half:], im[:half] - im[half:]], axis=0))
        re = jnp.concatenate([even[:half], odd[:half]], axis=0)
        im = jnp.concatenate([even[half:], odd[half:]], axis=0)
        far = [
            mul_right(jnp.concatenate([re[:, :half] + re[:, half:], im[:, :half] + im[:, half:]], axis=1), right[2]),
            mul_right(jnp.concatenate([re[:, :half] - re[:, half:], im[:, :half] - im[:, half:]], axis=1), right[3]),
        ]
        back = []
        for which, wave in enumerate(far):
            re, im = wave[:, :half], wave[:, half:]
            root = roots[p, :, which * half : which * half + half]
            factor = 1.0 - root * lax.rsqrt(re * re + im * im + smoothing)
            chi = jnp.concatenate([re * factor, im * factor], axis=1)
            back.append(mul_right(chi, right[which]))
        low, high = back[0] + back[1], back[0] - back[1]
        re = jnp.concatenate([low[:, :half], high[:, :half]], axis=1)
        im = jnp.concatenate([low[:, half:], high[:, half:]], axis=1)
        even = mul_left(left[2], jnp.concatenate([re[:half], im[:half]], axis=0))
        odd = mul_left(left[3], jnp.concatenate([re[half:], im[half:]], axis=0))
        low, high = even + odd, even - odd
        re = jnp.concatenate([low[:half], high[:half]], axis=0)
        im = jnp.concatenate([low[half:], high[half:]], axis=0)
        place(0, jnp.where(used, re * probe_r + im * probe_i, 0.0))
        place(1, jnp.where(used, im * probe_r - re * probe_i, 0.0))

    def start_rows(sweep, first, last):
        cells, slot = slice(first, last), slice(first - lo, last - lo)
        return [
            Send("up", grad.at[sweep, :, cells, 0:half], from_rows.at[sweep, 1, :, slot]),
            Send("down", grad.at[sweep, :, cells, half + width : full], from_rows.at[sweep, 0, :, slot]),
        ]

    def end_rows(sweep, first, last, copies):
        cells, slot = slice(first, last), slice(first - lo, last - lo)
        finish(copies)
        grad[sweep, :, cells, half:width] += from_rows[sweep, 0, :, slot]
        grad[sweep, :, cells, width : width + half] += from_rows[sweep, 1, :, slot]

    def start_side(sweep, side, first, last, slot):
        landing = from_cols.at[sweep, 1 if side == "left" else 0, :, slot : slot + last - first]
        return Send(side, grad.at[sweep, :, first:last, inner], landing)

    def step(sweep, first, last, exists=None, term=None):
        total = grad[sweep, :, first:last, inner]
        if term is not None:
            total = total + term
        new = ext[:, first:last, inner] - step_size * total
        return new if exists is None else jnp.where(exists, new, 0.0)

    split_lo, split_hi = half + lo, width + reach
    near = half + reach
    far_in = half + width - reach
    here_left, here_right = there["left"][0], there["right"][0]
    left_slots = [p for p in range(slots) if p % 2 == 0]
    right_slots = [p for p in range(slots) if p % 2 == 1]

    visit(0, left_slots[0])
    leftward.received()
    corners = send_rows(half + width, hi)
    for p in left_slots[1:]:
        visit(0, p)
    early_rows = start_rows(0, lo, split_lo)
    finish(corners)
    visit(0, right_slots[0])
    end_rows(0, lo, split_lo, early_rows)
    left_main = start_side(0, "left", lo, split_lo, 0)
    for p in right_slots[1:]:
        visit(0, p)
    rest_rows = start_rows(0, split_lo, near)
    edge_rows = start_rows(0, far_in, hi)
    middle_rows = start_rows(0, near, far_in)
    end_rows(0, split_lo, near, rest_rows)
    left_rest = start_side(0, "left", split_lo, near, half)
    end_rows(0, far_in, hi, edge_rows)
    right_rest = start_side(0, "right", far_in + half, hi, half)
    right_main = start_side(0, "right", far_in, far_in + half, 0)
    end_rows(0, near, far_in, middle_rows)
    leftward.sent()
    left_main.received()
    left_rest.received()
    right_rest.received()
    ext[:, split_lo:near, inner] = step(0, split_lo, near, None, from_cols[0, 0, :, half : 2 * reach])
    ext[:, near:far_in, inner] = step(0, near, far_in)
    ext[:, far_in : half + width, inner] = step(0, far_in, half + width, None, from_cols[0, 1, :, 0:reach])
    ext[:, half + width : hi, inner] = step(0, half + width, hi, here_right, from_cols[0, 1, :, reach : 2 * reach])
    finish(send_rows(split_lo, hi))

    visit(1, right_slots[0])
    right_main.received()
    ext[:, lo:half, inner] = step(0, lo, half, here_left, from_cols[0, 0, :, 0:reach])
    ext[:, half:split_lo, inner] = step(0, half, split_lo, None, from_cols[0, 0, :, reach:half])
    upright = send_rows(lo, split_lo)
    for p in right_slots[1:]:
        visit(1, p)
    late_rows = start_rows(1, split_hi, hi)
    finish(upright)
    visit(1, left_slots[0])
    end_rows(1, split_hi, hi, late_rows)
    right_last = start_side(1, "right", half + width, hi, 0)
    for p in left_slots[1:]:
        visit(1, p)
    edge_rows = start_rows(1, lo, half)
    middle_rows = start_rows(1, half, split_hi)
    end_rows(1, lo, half, edge_rows)
    left_last = start_side(1, "left", lo, half, 0)
    end_rows(1, half, split_hi, middle_rows)
    for part in (0, 1):
        ext[part, near:far_in, inner] -= step_size * grad[1, part, near:far_in, inner]
    right_last.received()
    ext[:, half:near, inner] = step(1, half, near, None, from_cols[1, 0, :, 0:reach])
    left_last.received()
    ext[:, far_in : half + width, inner] = step(1, far_in, half + width, None, from_cols[1, 1, :, 0:reach])
    out_re[...] = ext[0, inner, inner]
    out_im[...] = ext[1, inner, inner]
    for copy in (left_main, left_rest, right_rest, right_main, right_last, left_last):
        copy.sent()


def turn(turned_re, turned_im, final_re, final_im):
    final_re[...] = turned_re[...].T
    final_im[...] = turned_im[...].T


def shards(rows, cols, object_re, object_im, probe_re, probe_im, intensity, offsets, counts):
    width = probe_re.shape[0]
    half = width // 2
    reach = half - half // 2 + half // 8
    slots = intensity.shape[2]
    left, right = split_tables(width)
    f32 = jnp.float32
    vmem = pl.BlockSpec(memory_space=pltpu.VMEM)
    smem = pl.BlockSpec(memory_space=pltpu.SMEM)
    tile = jax.ShapeDtypeStruct(object_re.shape, f32)
    turned = jax.ShapeDtypeStruct(object_re.shape[::-1], f32)
    turned_re, turned_im = pl.pallas_call(
        functools.partial(kernel, rows, cols),
        out_shape=(turned, turned),
        in_specs=[smem, smem] + [vmem] * 4 + [pl.BlockSpec(memory_space=pl.ANY)] * 3,
        out_specs=(vmem, vmem),
        scratch_shapes=[
            pltpu.VMEM((2, 2 * width, 2 * width), f32),
            pltpu.VMEM((ITERS, 2, 2 * width, 2 * width), f32),
            pltpu.VMEM((slots, 2, width, width), f32),
            pltpu.VMEM((slots, width, width), f32),
            pltpu.VMEM((2, width, half), f32),
            pltpu.VMEM((width, half), f32),
            pltpu.VMEM((ITERS, 2, 2, width + 2 * reach, half), f32),
            pltpu.VMEM((ITERS, 2, 2, 2 * reach, width), f32),
            pltpu.VMEM(intensity.shape[2:], f32),
            pltpu.VMEM(left.shape, jnp.bfloat16),
            pltpu.VMEM(right.shape, jnp.bfloat16),
            pltpu.SemaphoreType.DMA((40,)),
            pltpu.SemaphoreType.DMA((40,)),
            pltpu.SemaphoreType.DMA((3,)),
        ],
        compiler_params=pltpu.CompilerParams(
            collective_id=0, has_side_effects=True, vmem_limit_bytes=56 * 1024 * 1024
        ),
    )(
        offsets[0, 0], counts[0], object_re, object_im, probe_re, probe_im, intensity[0, 0],
        jnp.asarray(left), jnp.asarray(right),
    )
    return pl.pallas_call(turn, out_shape=(tile, tile), in_specs=[vmem] * 2, out_specs=(vmem, vmem))(
        turned_re, turned_im
    )


def solution(mesh):
    return jax.shard_map(
        functools.partial(shards, mesh.shape["row"], mesh.shape["col"]),
        mesh=mesh,
        in_specs=(
            P("row", "col"),
            P("row", "col"),
            P(),
            P(),
            P("row", "col", None, None, None),
            P("row", "col", None, None),
            P("row", "col"),
        ),
        out_specs=(P("row", "col"), P("row", "col")),
        check_vma=False,
    )
```
